32 devices in a mesh: leaf: 8 (over y, x, core), col: 4 (over z).
Axes of the slice: x: 2, y: 2, z: 4, core: 2. Of those that a mesh axis runs over, the one named last changes fastest.
Arguments:
- right_side: float32 [31, 2560, 256], P(None, 'leaf'), may hold values from -6 to 6
- reciprocal_pivot_matrix: bfloat16 [31, 2560, 2560], P(None, 'col', 'leaf'), as said below
- panels: bfloat16 [98, 2560, 2560], P(None, 'leaf', 'col'), may hold values from -0.03125 to 0.03125
- parent: int32 [31], replicated, may hold values from 16 to 30, as said below
Outputs:
- solution: float32 [31, 2560, 256], P(None, 'leaf')
The draws below stay inside these ranges and needn't reach their ends.
Inputs may be any that keep to these rules, and one draw needn't show every extreme that they name: Supernodes 0 to 15 have parents among 16 to 23, 16 to 23 among 24 to 27, 24 to 27 among 28 and 29, 28 and 29 have parent 30, and entry 30 is 30 itself; each supernode of levels 1 to 4 is the parent of exactly two supernodes of the level below. `reciprocal_pivot_matrix`: each block is lower triangular with a positive diagonal.
All inputs are finite; a program needn't handle non-finite values.
Results may differ from the reference program's by a relative error of at most 0.03.
Values may be sent and summed in bfloat16 or wider, within the bound.
A program may use at most 192 MiB of HBM per device.

```python
import math
import jax
import jax.numpy as jnp
from jax import lax

B = 2560
NRHS = 256
NS = 31
NP = 98
N_LEAF = 8
N_COL = 4


def draw_reciprocal_pivot_matrix(key, part):
    lower_key = jax.random.fold_in(key, 11)
    diag_key = jax.random.fold_in(key, 12)
    row_index = lax.broadcasted_iota(jnp.int32, (NS, B, B), 1)
    columns = lax.broadcasted_iota(jnp.int32, (NS, B, B), 2)
    spread = jax.random.normal(lower_key, (NS, B, B), jnp.float32) * (0.5 / math.sqrt(B))
    scales = jax.random.uniform(diag_key, (NS, B, 1), jnp.float32, 0.5, 1.5)
    entries = jnp.where(columns < row_index, spread, jnp.where(columns == row_index, scales, 0.0))
    return entries.astype(jnp.bfloat16)


def draw_parent(key, part):
    division_count = []
    offset_node = 0
    for tree_level, node_count in enumerate((16, 8, 4, 2)):
        shuffled = jax.random.permutation(jax.random.fold_in(key, 21 + tree_level), node_count)
        division_count.append(offset_node + node_count + shuffled // 2)
        offset_node = offset_node + node_count
    division_count.append(jnp.full((1,), NS - 1, jnp.int32))
    return jnp.concatenate([piece.astype(jnp.int32) for piece in division_count])


def shard_levels(key, dims, pieces, low, largest):
    gain = 1.0
    for axis_at, parts in pieces:
        heights = jax.random.uniform(jax.random.fold_in(jax.random.fold_in(key, 6), axis_at), (parts,), jnp.float32, low / len(pieces), largest / len(pieces))
        gain = gain * jnp.repeat(jnp.exp(heights), dims[axis_at] // parts).reshape((-1,) + (1,) * (len(dims) - 1 - axis_at))
    return gain


def scatter_about(own_key, extent, scale, most, cuts=(), kind=jnp.bfloat16):
    drawn = jax.random.normal(own_key, extent, jnp.float32) * scale
    if len(cuts) > 0:
        drawn = shard_levels(own_key, extent, cuts, -0.22, 0.18) * drawn
    return jnp.clip(drawn, min=-most, max=most).astype(kind)


def setup_inputs(seed: int = 0) -> dict:
    key_of = jax.random.split(jax.random.key(seed), 5)
    right_side = scatter_about(key_of[0], (NS, B, NRHS), 1.0, 6.0, ((1, 8),), jnp.float32)
    reciprocal_pivot_matrix = draw_reciprocal_pivot_matrix(jax.random.fold_in(key_of[4], 71), 0)
    panels = scatter_about(key_of[2], (NP, B, B), (16 * B) ** -0.5, 0.03125, ((1, 8), (2, 4)))
    parent = draw_parent(jax.random.fold_in(key_of[4], 71), 0)
    return {"right_side": right_side, "reciprocal_pivot_matrix": reciprocal_pivot_matrix, "panels": panels, "parent": parent}


level_starts = (0, 16, 24, 28, 30)
level_counts = (16, 8, 4, 2, 1)


def pair_table():
    sources = []
    distances = []
    for tree_level in range(5):
        for tree_vertex in range(level_starts[tree_level], level_starts[tree_level] + level_counts[tree_level]):
            for distance in range(1, 5 - tree_level):
                sources.append(tree_vertex)
                distances.append(distance)
    return sources, distances


def node_level(tree_vertex):
    deepest = 0
    for tree_level in range(5):
        if level_starts[tree_level] <= tree_vertex:
            deepest = tree_level
    return deepest


def pair_ancestors(parent):
    sources, distances = pair_table()
    climbed = [jnp.arange(parent.shape[0], dtype=jnp.int32)]
    for distance in range(4):
        climbed.append(parent[climbed[-1]])
    return jnp.stack([climbed[distance][source_node] for source_node, distance in zip(sources, distances)]).astype(jnp.int32)


def rounded(values):
    return lax.optimization_barrier(values.astype(jnp.bfloat16)).astype(jnp.float32)


def reference(right_side, reciprocal_pivot_matrix, panels, parent):
    sources, distances = pair_table()
    ancestor = pair_ancestors(parent)
    cluster_breadth = right_side.shape[1]
    load_vector_count = right_side.shape[2]
    bottom_frontal_tile = cluster_breadth // N_LEAF
    col_block = cluster_breadth // N_COL
    forward_full = {}
    forward_half = {}
    for tree_level in range(5):
        start_node = level_starts[tree_level]
        node_count = level_counts[tree_level]
        reduced = right_side[start_node:start_node + node_count]
        if tree_level > 0:
            waiting_updates = jnp.zeros((node_count, N_COL, cluster_breadth, load_vector_count), jnp.float32)
            slots = jnp.arange(node_count, dtype=jnp.int32) + start_node
            for node_pairing in range(len(sources)):
                if node_level(sources[node_pairing]) + distances[node_pairing] == tree_level:
                    onehot = (slots == ancestor[node_pairing]).astype(jnp.float32)
                    product = jnp.einsum("ajc,jcr->jar", panels[node_pairing].astype(jnp.float32).reshape(cluster_breadth, N_COL, col_block), forward_half[sources[node_pairing]].astype(jnp.float32).reshape(N_COL, col_block, load_vector_count))
                    waiting_updates = waiting_updates + onehot[:, None, None, None] * product[None]
            reduced = reduced - jnp.sum(rounded(waiting_updates), axis=1)
        reduced_portion = lax.optimization_barrier(reduced.astype(jnp.bfloat16))
        for initial_position in range(node_count):
            tree_vertex = start_node + initial_position
            division_count = jnp.einsum("cfw,fwx->fcx", reciprocal_pivot_matrix[tree_vertex].astype(jnp.float32).reshape(cluster_breadth, N_LEAF, bottom_frontal_tile), reduced_portion[initial_position].astype(jnp.float32).reshape(N_LEAF, bottom_frontal_tile, load_vector_count))
            forward_value = jnp.sum(rounded(division_count), axis=0)
            forward_full[tree_vertex] = forward_value
            forward_half[tree_vertex] = lax.optimization_barrier(forward_value.astype(jnp.bfloat16))
    solution_half = jnp.zeros((NS, cluster_breadth, load_vector_count), jnp.bfloat16)
    results = [None] * 5
    for tree_level in (4, 3, 2, 1, 0):
        start_node = level_starts[tree_level]
        node_count = level_counts[tree_level]
        outputs = []
        for initial_position in range(node_count):
            tree_vertex = start_node + initial_position
            corrected = forward_full[tree_vertex]
            if tree_level < 4:
                waiting_updates = jnp.zeros((N_LEAF, cluster_breadth, load_vector_count), jnp.float32)
                for node_pairing in range(len(sources)):
                    if sources[node_pairing] == tree_vertex:
                        upper_node = solution_half[ancestor[node_pairing]]
                        waiting_updates = waiting_updates + jnp.einsum("uwk,uwn->ukn", panels[node_pairing].astype(jnp.float32).reshape(N_LEAF, bottom_frontal_tile, cluster_breadth), upper_node.astype(jnp.float32).reshape(N_LEAF, bottom_frontal_tile, load_vector_count))
                corrected = corrected - jnp.sum(rounded(waiting_updates), axis=0)
            corrected_half = lax.optimization_barrier(corrected.astype(jnp.bfloat16))
            division_count = jnp.einsum("jca,jcr->jar", reciprocal_pivot_matrix[tree_vertex].astype(jnp.float32).reshape(N_COL, col_block, cluster_breadth), corrected_half.astype(jnp.float32).reshape(N_COL, col_block, load_vector_count))
            outputs.append(jnp.sum(rounded(division_count), axis=0))
        level_solution = jnp.stack(outputs)
        solution_half = solution_half.at[start_node:start_node + node_count].set(lax.optimization_barrier(level_solution.astype(jnp.bfloat16)))
        results[tree_level] = level_solution
    return jnp.concatenate(results, axis=0)
```

```python
import functools

import jax
import jax.numpy as jnp
import numpy as np
from jax import lax
from jax.experimental import pallas as pl
from jax.experimental.pallas import tpu as pltpu
from jax.sharding import PartitionSpec as P

MESH = pl.DeviceIdType.MESH
VMEM_BYTES = 58 * 2**20
LAG = 2


level_starts = (0, 16, 24, 28, 30)
level_counts = (16, 8, 4, 2, 1)


def pair_table():
    sources = []
    distances = []
    for tree_level in range(5):
        for tree_vertex in range(
            level_starts[tree_level], level_starts[tree_level] + level_counts[tree_level]
        ):
            for distance in range(1, 5 - tree_level):
                sources.append(tree_vertex)
                distances.append(distance)
    return (sources, distances)


def node_level(tree_vertex):
    deepest = 0
    for tree_level in range(5):
        if level_starts[tree_level] <= tree_vertex:
            deepest = tree_level
    return deepest


def pair_offset(tree_level):
    initial_position = 0
    for lower in range(tree_level):
        initial_position = initial_position + level_counts[lower] * (4 - lower)
    return initial_position


def pair_ancestors(parent):
    sources, distances = pair_table()
    climbed = [jnp.arange(parent.shape[0], dtype=jnp.int32)]
    for distance in range(4):
        climbed.append(parent[climbed[-1]])
    return jnp.stack(
        [climbed[distance][source_node] for source_node, distance in zip(sources, distances)]
    )


def forward_products(panel_local, forward_stack, ancestor, pair_list, start_node, node_count):
    sources, distances = pair_table()
    chosen = np.array(pair_list, dtype=np.int32)
    feeders = np.array([sources[node_pairing] for node_pairing in pair_list], dtype=np.int32)
    products = jnp.einsum(
        "sjv,svk->sjk",
        panel_local[chosen],
        forward_stack[feeders],
        preferred_element_type=jnp.float32,
    )
    slots = jnp.arange(node_count, dtype=jnp.int32) + start_node
    onehot = (slots[:, None] == ancestor[chosen][None, :]).astype(jnp.float32)
    return jnp.einsum("kp,par->kar", onehot, products, precision=lax.Precision.HIGHEST)


def solve(right_side, diag_local, panel_local, ancestor):
    sources, distances = pair_table()
    node_total = right_side.shape[0]
    load_vector_count = right_side.shape[2]
    col_rows = diag_local.shape[1]
    leaf_rows = diag_local.shape[2]
    forward_stack = jnp.zeros((node_total, col_rows, load_vector_count), jnp.bfloat16)
    forward_levels = [None] * 5
    for tree_level in range(5):
        start_node = level_starts[tree_level]
        node_count = level_counts[tree_level]
        reduced = right_side[start_node : start_node + node_count]
        if tree_level > 0:
            arriving = [
                node_pairing
                for node_pairing in range(len(sources))
                if node_level(sources[node_pairing]) + distances[node_pairing] == tree_level
            ]
            partial_value = forward_products(
                panel_local, forward_stack, ancestor, arriving, start_node, node_count
            )
            reduced = reduced - lax.psum(partial_value.astype(jnp.bfloat16), "col").astype(
                jnp.float32
            )
        division_count = jnp.einsum(
            "kcl,klr->kcr",
            diag_local[start_node : start_node + node_count],
            reduced.astype(jnp.bfloat16),
            preferred_element_type=jnp.float32,
        )
        forward_value = lax.psum(division_count.astype(jnp.bfloat16), "leaf").astype(jnp.float32)
        forward_levels[tree_level] = forward_value
        forward_stack = forward_stack.at[start_node : start_node + node_count].set(
            forward_value.astype(jnp.bfloat16)
        )
    solution_stack = jnp.zeros((node_total, leaf_rows, load_vector_count), jnp.bfloat16)
    results = [None] * 5
    for tree_level in (4, 3, 2, 1, 0):
        start_node = level_starts[tree_level]
        node_count = level_counts[tree_level]
        corrected = forward_levels[tree_level]
        if tree_level < 4:
            initial_position = pair_offset(tree_level)
            span_pairs = node_count * (4 - tree_level)
            upper_node = solution_stack[ancestor[initial_position : initial_position + span_pairs]]
            products = jnp.einsum(
                "boj,boh->bjh",
                panel_local[initial_position : initial_position + span_pairs],
                upper_node,
                preferred_element_type=jnp.float32,
            )
            partial_value = jnp.sum(
                products.reshape(node_count, 4 - tree_level, col_rows, load_vector_count), axis=1
            )
            corrected = corrected - lax.psum(partial_value.astype(jnp.bfloat16), "leaf").astype(
                jnp.float32
            )
        division_count = jnp.einsum(
            "kcl,kcr->klr",
            diag_local[start_node : start_node + node_count],
            corrected.astype(jnp.bfloat16),
            preferred_element_type=jnp.float32,
        )
        solution = lax.psum(division_count.astype(jnp.bfloat16), "col").astype(jnp.float32)
        results[tree_level] = solution
        solution_stack = solution_stack.at[start_node : start_node + node_count].set(
            solution.astype(jnp.bfloat16)
        )
    return jnp.concatenate(results, axis=0)


def bf16(value):
    return value.astype(jnp.bfloat16)


def f32(value):
    return value.astype(jnp.float32)


def send(src, dst, sems, at, device):
    return pltpu.make_async_remote_copy(
        src_ref=src,
        dst_ref=dst,
        send_sem=sems[0].at[at],
        recv_sem=sems[1].at[at],
        device_id=device,
        device_id_type=MESH,
    )


class Leaf:
    def __init__(self, part, result, finish, half_in, first, first_in, second, second_in, sems):
        self.part, self.result, self.finish = part, result, finish
        self.half_in, self.first, self.first_in = half_in, first, first_in
        self.second, self.second_in, self.sems = second, second_in, sems
        me = lax.axis_index("leaf")
        self.core = me % 2
        self.sibling = {"leaf": me + 1 - 2 * self.core}
        self.along_x = {"leaf": me + 2 - 4 * ((me // 2) % 2)}
        self.along_y = {"leaf": me + 4 - 8 * (me // 4)}
        self.half = part.shape[1] // 2
        self.quarter = self.half // 2
        self.mine = pl.ds(self.core * self.half, self.half)
        self.other = pl.ds((1 - self.core) * self.half, self.half)

    def neighbours(self):
        return (self.sibling, self.along_x, self.along_y)

    def scatter(self, k):
        return send(self.part.at[k, self.other], self.half_in.at[k], self.sems[0], k, self.sibling)

    def exchange(self, k, step):
        source, target = ((self.first, self.first_in), (self.second, self.second_in))[step]
        low, high = pl.ds(0, self.quarter), pl.ds(self.quarter, self.quarter)
        ways = (self.along_x, self.along_y) if step == 0 else (self.along_y, self.along_x)
        return (
            send(source.at[k, low], target.at[k, low], self.sems[1 + 2 * step], k, ways[0]),
            send(source.at[k, high], target.at[k, high], self.sems[2 + 2 * step], k, ways[1]),
        )

    def gather(self, k):
        return send(self.result.at[k, self.mine], self.result.at[k, self.mine], self.sems[5], k, self.sibling)

    def stage_first(self, k):
        self.scatter(k).wait_recv()
        self.first[k] = bf16(f32(self.part[k, self.mine]) + f32(self.half_in[k]))
        for copy in self.exchange(k, 0):
            copy.start()

    def stage_second(self, k):
        for copy in self.exchange(k, 0):
            copy.wait_recv()
        self.second[k] = bf16(f32(self.first[k]) + f32(self.first_in[k]))
        for copy in self.exchange(k, 1):
            copy.start()

    def stage_result(self, k):
        for copy in self.exchange(k, 1):
            copy.wait_recv()
        total = f32(self.second[k]) + f32(self.second_in[k])
        self.result[k, self.mine] = self.finish(k, self.mine, total)
        self.gather(k).start()

    def stage_gathered(self, k):
        self.gather(k).wait_recv()

    def drain(self, k):
        self.scatter(k).wait_send()
        for copy in self.exchange(k, 0) + self.exchange(k, 1):
            copy.wait_send()
        self.gather(k).wait_send()


class Col:
    def __init__(self, part, result, arrived, joined, joined_in, sems):
        self.part, self.result, self.arrived = part, result, arrived
        self.joined, self.joined_in, self.sems = joined, joined_in, sems
        me = lax.axis_index("col")
        self.inner = jnp.logical_or(me == 1, me == 2)
        self.end = jnp.logical_or(me == 0, me == 3)
        self.end_partner = {"col": (me // 2) + 1}
        self.inner_partner = {"col": 3 - me}
        self.outer = {"col": (me // 2) * 3}

    def greet(self, barrier):
        @pl.when(self.end)
        def _():
            pl.semaphore_signal(barrier, inc=1, device_id=self.end_partner, device_id_type=MESH)

        @pl.when(self.inner)
        def _():
            pl.semaphore_signal(barrier, inc=1, device_id=self.inner_partner, device_id_type=MESH)
            pl.semaphore_signal(barrier, inc=1, device_id=self.outer, device_id_type=MESH)

    def to_inner(self, k):
        return send(self.part.at[k], self.arrived.at[k], self.sems[0], k, self.end_partner)

    def across(self, k):
        return send(self.joined.at[k], self.joined_in.at[k], self.sems[1], k, self.inner_partner)

    def to_end(self, k):
        return send(self.result.at[k], self.result.at[k], self.sems[2], k, self.outer)

    def stage_start(self, k):
        @pl.when(self.end)
        def _():
            self.to_inner(k).start()

    def stage_join(self, k):
        @pl.when(self.inner)
        def _():
            self.to_inner(k).wait_recv()
            self.joined[k] = bf16(f32(self.part[k]) + f32(self.arrived[k]))
            self.across(k).start()

    def stage_sum(self, k):
        @pl.when(self.inner)
        def _():
            self.across(k).wait_recv()
            self.result[k] = bf16(f32(self.joined[k]) + f32(self.joined_in[k]))
            self.to_end(k).start()

    def stage_end(self, k):
        @pl.when(self.end)
        def _():
            self.to_end(k).wait_recv()

    def drain(self, k):
        @pl.when(self.end)
        def _():
            self.to_inner(k).wait_send()

        @pl.when(self.inner)
        def _():
            self.across(k).wait_send()
            self.to_end(k).wait_send()


def enter(leaf, col):
    barrier = pltpu.get_barrier_semaphore()
    count = 0
    if leaf is not None:
        for neighbour in leaf.neighbours():
            pl.semaphore_signal(barrier, inc=1, device_id=neighbour, device_id_type=MESH)
        count = 3
    if col is None:
        pl.semaphore_wait(barrier, count)
    else:
        col.greet(barrier)

        @pl.when(col.end)
        def _():
            pl.semaphore_wait(barrier, count + 1)

        @pl.when(col.inner)
        def _():
            pl.semaphore_wait(barrier, count + 2)


def staged(count, stages):
    last = max(lag for lag, _ in stages)

    def body(step, carry):
        for lag, stage in reversed(stages):
            node = step - lag

            @pl.when(jnp.logical_and(node >= 0, node < count))
            def _(stage=stage, node=node):
                stage(node)

        return carry

    lax.fori_loop(0, count + last, body, 0)


def each(count, stage):
    def body(k, carry):
        stage(k)
        return carry

    lax.fori_loop(0, count, body, 0)


def pair_sems(refs, count):
    return [(refs[2 * at], refs[2 * at + 1]) for at in range(count)]


def forward_kernel(start, count, has_update, *refs):
    refs = list(refs)
    take = lambda number: [refs.pop(0) for _ in range(number)]
    update = take(1)[0] if has_update else None
    right_hbm, diag_hbm, y_ref, right, diag, load_sem = take(6)
    part, half_in, first, first_in, second, second_in = take(6)
    leaf_sems = pair_sems(take(12), 6)
    leaf = Leaf(
        part, y_ref, lambda k, rows, total: bf16(total), half_in, first, first_in, second, second_in, leaf_sems
    )
    col = None
    if has_update:
        summed, arrived, joined, joined_in = take(4)
        col = Col(update, summed, arrived, joined, joined_in, pair_sems(take(6), 3))
    loads = [
        pltpu.make_async_copy(right_hbm.at[pl.ds(start, count)], right, load_sem.at[0]),
        pltpu.make_async_copy(diag_hbm.at[pl.ds(start, count)], diag, load_sem.at[1]),
    ]
    for load in loads:
        load.start()
    enter(leaf, col)
    if has_update:
        each(count, col.stage_start)
    for load in loads:
        load.wait()

    def divide(k):
        reduced = right[k]
        if has_update:
            col.stage_end(k)
            reduced = reduced - f32(summed[k])
        part[k] = bf16(jnp.dot(diag[k], bf16(reduced), preferred_element_type=jnp.float32))
        leaf.scatter(k).start()

    stages = []
    lag = 0
    if has_update:
        stages += [(0, col.stage_join), (LAG, col.stage_sum)]
        lag = LAG + 1
    stages += [
        (lag, divide),
        (lag + 1, leaf.stage_first),
        (lag + 1 + LAG, leaf.stage_second),
        (lag + 1 + 2 * LAG, leaf.stage_result),
    ]
    staged(count, stages)
    each(count, leaf.stage_gathered)
    each(count, leaf.drain)
    if has_update:
        each(count, col.drain)


def backward_kernel(start, count, has_update, *refs):
    refs = list(refs)
    take = lambda number: [refs.pop(0) for _ in range(number)]
    update = take(1)[0] if has_update else None
    y_ref, diag_hbm, x_ref, diag, load_sem, part, arrived, joined, joined_in = take(9)
    col = Col(part, x_ref, arrived, joined, joined_in, pair_sems(take(6), 3))
    leaf = None
    if has_update:
        z_ref, half_in, first, first_in, second, second_in = take(6)

        def finish(k, rows, total):
            return bf16(f32(y_ref[k, rows]) - total)

        leaf = Leaf(
            update, z_ref, finish, half_in, first, first_in, second, second_in, pair_sems(take(12), 6)
        )
    load = pltpu.make_async_copy(diag_hbm.at[pl.ds(start, count)], diag, load_sem.at[0])
    load.start()
    enter(leaf, col)
    if has_update:
        each(count, lambda k: leaf.scatter(k).start())
    load.wait()

    def divide(k):
        if has_update:
            leaf.stage_gathered(k)
            corrected = z_ref[k]
        else:
            corrected = y_ref[k]
        part[k] = bf16(
            lax.dot_general(
                diag[k], corrected, (((0,), (0,)), ((), ())), preferred_element_type=jnp.float32
            )
        )
        col.stage_start(k)

    stages = []
    lag = 0
    if has_update:
        stages += [
            (0, leaf.stage_first),
            (LAG, leaf.stage_second),
            (2 * LAG, leaf.stage_result),
        ]
        lag = 2 * LAG + 1
    stages += [(lag, divide), (lag + LAG, col.stage_join), (lag + 2 * LAG, col.stage_sum)]
    staged(count, stages)
    each(count, col.stage_end)
    each(count, col.drain)
    if has_update:
        each(count, leaf.drain)


def leaf_scratch(count, rows, rhs):
    half = pltpu.VMEM((count, rows // 2, rhs), jnp.bfloat16)
    return [half] * 5


def sem_scratch(count, number):
    return [pltpu.SemaphoreType.DMA((count,))] * (2 * number)


def cost(flops, moved):
    return pl.CostEstimate(flops=flops, bytes_accessed=moved, transcendentals=0)


def forward_level(level, update, right_side, diag):
    start, count = level_starts[level], level_counts[level]
    rows, depth = diag.shape[1], diag.shape[2]
    rhs = right_side.shape[2]
    has_update = update is not None
    block = pltpu.VMEM((count, depth, rhs), jnp.bfloat16)
    scratch = [
        pltpu.VMEM((count, depth, rhs), jnp.float32),
        pltpu.VMEM((count, rows, depth), jnp.bfloat16),
        pltpu.SemaphoreType.DMA((2,)),
        pltpu.VMEM((count, rows, rhs), jnp.bfloat16),
    ]
    scratch += leaf_scratch(count, rows, rhs) + sem_scratch(count, 6)
    if has_update:
        scratch += [block] * 4 + sem_scratch(count, 3)
    vmem = pl.BlockSpec(memory_space=pltpu.VMEM)
    anywhere = pl.BlockSpec(memory_space=pl.ANY)
    return pl.pallas_call(
        functools.partial(forward_kernel, start, count, has_update),
        out_shape=jax.ShapeDtypeStruct((count, rows, rhs), jnp.bfloat16),
        in_specs=[vmem] * has_update + [anywhere] * 2,
        out_specs=vmem,
        scratch_shapes=scratch,
        name=f"forward_level_{level}",
        cost_estimate=cost(2 * count * rows * depth * rhs, 2 * count * rows * (depth + rhs)),
        compiler_params=pltpu.CompilerParams(
            collective_id=level, has_side_effects=True, vmem_limit_bytes=VMEM_BYTES
        ),
    )(*([update] * has_update), right_side, diag)


def backward_level(level, update, forward_value, diag):
    start, count = level_starts[level], level_counts[level]
    rows, depth = diag.shape[1], diag.shape[2]
    rhs = forward_value.shape[2]
    has_update = update is not None
    block = pltpu.VMEM((count, depth, rhs), jnp.bfloat16)
    scratch = [pltpu.VMEM((count, rows, depth), jnp.bfloat16), pltpu.SemaphoreType.DMA((1,))]
    scratch += [block] * 4 + sem_scratch(count, 3)
    if has_update:
        scratch += [pltpu.VMEM((count, rows, rhs), jnp.bfloat16)]
        scratch += leaf_scratch(count, rows, rhs) + sem_scratch(count, 6)
    vmem = pl.BlockSpec(memory_space=pltpu.VMEM)
    anywhere = pl.BlockSpec(memory_space=pl.ANY)
    return pl.pallas_call(
        functools.partial(backward_kernel, start, count, has_update),
        out_shape=jax.ShapeDtypeStruct((count, depth, rhs), jnp.bfloat16),
        in_specs=[vmem] * has_update + [vmem, anywhere],
        out_specs=vmem,
        scratch_shapes=scratch,
        name=f"backward_level_{level}",
        cost_estimate=cost(2 * count * rows * depth * rhs, 2 * count * rows * (depth + rhs)),
        compiler_params=pltpu.CompilerParams(
            collective_id=5 + level, has_side_effects=True, vmem_limit_bytes=VMEM_BYTES
        ),
    )(*([update] * has_update), forward_value, diag)


def forward_update(level, panels, values, order, feeders):
    count = level_counts[level]
    rows, depth = panels.shape[1], panels.shape[2]
    rhs = values[0].shape[2]
    lows = [sum(2 ** (level - lower) for lower in range(q)) for q in range(level + 1)]
    per_node = lows[level]
    base = sum(
        level_counts[upper] * sum(2 ** (upper - lower) for lower in range(upper))
        for upper in range(1, level)
    )

    def body(order_ref, feeders_ref, panel, *refs):
        sources, out, total = refs[:level], refs[level], refs[level + 1]
        m = pl.program_id(1)

        @pl.when(m == 0)
        def _():
            total[...] = jnp.zeros_like(total)

        for q in range(level):

            @pl.when(jnp.logical_and(m >= lows[q], m < lows[q + 1]))
            def _(q=q):
                total[...] += jnp.dot(panel[0], sources[q][0], preferred_element_type=jnp.float32)

        @pl.when(m == per_node - 1)
        def _():
            out[0] = bf16(total[...])

    def panel_at(k, m, order_ref, feeders_ref):
        return (order_ref[base + k * per_node + m], 0, 0)

    def source_at(q):
        def at(k, m, order_ref, feeders_ref):
            near = jnp.minimum(jnp.maximum(m, lows[q]), lows[q + 1] - 1)
            return (feeders_ref[base + k * per_node + near] - level_starts[q], 0, 0)

        return at

    return pl.pallas_call(
        body,
        grid_spec=pltpu.PrefetchScalarGridSpec(
            num_scalar_prefetch=2,
            grid=(count, per_node),
            in_specs=[pl.BlockSpec((1, rows, depth), panel_at)]
            + [pl.BlockSpec((1, depth, rhs), source_at(q)) for q in range(level)],
            out_specs=pl.BlockSpec((1, rows, rhs), lambda k, m, *_: (k, 0, 0)),
            scratch_shapes=[pltpu.VMEM((rows, rhs), jnp.float32)],
        ),
        out_shape=jax.ShapeDtypeStruct((count, rows, rhs), jnp.bfloat16),
        name=f"forward_update_{level}",
        cost_estimate=cost(
            2 * count * per_node * rows * depth * rhs, 2 * count * per_node * depth * (rows + rhs)
        ),
        compiler_params=pltpu.CompilerParams(vmem_limit_bytes=VMEM_BYTES),
    )(order, feeders, panels, *values[:level])


def backward_update(level, panels, solutions, ancestor):
    count = level_counts[level]
    rows, depth = panels.shape[1], panels.shape[2]
    rhs = solutions[4].shape[2]
    distances = 4 - level
    base = pair_offset(level)

    def body(ancestor_ref, *refs):
        total = None
        for d in range(distances):
            product = lax.dot_general(
                refs[d][0],
                refs[distances + d][0],
                (((0,), (0,)), ((), ())),
                preferred_element_type=jnp.float32,
            )
            total = product if total is None else total + product
        refs[2 * distances][0] = bf16(total)

    def panel_at(d):
        return lambda k, ancestor_ref: (base + k * distances + d, 0, 0)

    def upper_at(d):
        above = level + 1 + d
        return lambda k, ancestor_ref: (
            ancestor_ref[base + k * distances + d] - level_starts[above],
            0,
            0,
        )

    return pl.pallas_call(
        body,
        grid_spec=pltpu.PrefetchScalarGridSpec(
            num_scalar_prefetch=1,
            grid=(count,),
            in_specs=[pl.BlockSpec((1, rows, depth), panel_at(d)) for d in range(distances)]
            + [pl.BlockSpec((1, rows, rhs), upper_at(d)) for d in range(distances)],
            out_specs=pl.BlockSpec((1, depth, rhs), lambda k, _: (k, 0, 0)),
        ),
        out_shape=jax.ShapeDtypeStruct((count, depth, rhs), jnp.bfloat16),
        name=f"backward_update_{level}",
        cost_estimate=cost(
            2 * count * distances * rows * depth * rhs, 2 * count * distances * rows * (depth + rhs)
        ),
        compiler_params=pltpu.CompilerParams(vmem_limit_bytes=VMEM_BYTES),
    )(ancestor, *([panels] * distances), *[solutions[level + 1 + d] for d in range(distances)])


def pairs_by_ancestor(parent):
    nodes = jnp.arange(parent.shape[0], dtype=jnp.int32)
    climbed = [parent]
    for _ in range(3):
        hit = climbed[-1][:, None] == nodes[None, :]
        climbed.append(jnp.sum(jnp.where(hit, parent[None, :], 0), axis=1))
    above = jnp.stack(climbed, axis=1)
    ancestor = jnp.concatenate(
        [
            above[level_starts[q] : level_starts[q] + level_counts[q], : 4 - q].reshape(-1)
            for q in range(4)
        ]
    )
    sources = jnp.asarray(np.array(pair_table()[0], dtype=np.int32))
    total = sources.shape[0]
    here = jnp.arange(total, dtype=jnp.int32)
    key = ancestor * total + here
    place = jnp.sum((key[None, :] < key[:, None]).astype(jnp.int32), axis=1)
    hit = place[None, :] == here[:, None]
    order = jnp.sum(jnp.where(hit, here[None, :], 0), axis=1)
    feeders = jnp.sum(jnp.where(hit, sources[None, :], 0), axis=1)
    return ancestor, order, feeders


def shards(right_side, diag, panels, parent):
    ancestor, order, feeders = pairs_by_ancestor(parent)
    values = []
    for level in range(5):
        update = forward_update(level, panels, values, order, feeders) if level else None
        values.append(forward_level(level, update, right_side, diag))
    solutions = [None] * 5
    for level in (4, 3, 2, 1, 0):
        update = backward_update(level, panels, solutions, ancestor) if level < 4 else None
        solutions[level] = backward_level(level, update, values[level], diag)
    return jnp.concatenate([f32(value) for value in solutions], axis=0)


def shards_any(right_side, reciprocal_pivot_matrix, panels, parent):
    ancestor = pair_ancestors(parent)
    return solve(right_side, reciprocal_pivot_matrix, panels, ancestor)


def solution(mesh):
    kernels = mesh.shape["leaf"] == 8 and mesh.shape["col"] == 4
    return jax.shard_map(
        shards if kernels else shards_any,
        mesh=mesh,
        in_specs=(P(None, "leaf", None), P(None, "col", "leaf"), P(None, "leaf", "col"), P()),
        out_specs=P(None, "leaf", None),
        check_vma=False,
    )
```

```python
import functools

import jax
import jax.numpy as jnp
import numpy as np
from jax import lax
from jax.experimental import pallas as pl
from jax.experimental.pallas import tpu as pltpu
from jax.sharding import PartitionSpec as P

MESH = pl.DeviceIdType.MESH
VMEM_BYTES = 58 * 2**20
LAG = 2
SPLIT = 2


level_starts = (0, 16, 24, 28, 30)
level_counts = (16, 8, 4, 2, 1)


def pair_table():
    sources = []
    distances = []
    for tree_level in range(5):
        for tree_vertex in range(
            level_starts[tree_level], level_starts[tree_level] + level_counts[tree_level]
        ):
            for distance in range(1, 5 - tree_level):
                sources.append(tree_vertex)
                distances.append(distance)
    return (sources, distances)


def node_level(tree_vertex):
    deepest = 0
    for tree_level in range(5):
        if level_starts[tree_level] <= tree_vertex:
            deepest = tree_level
    return deepest


def pair_offset(tree_level):
    initial_position = 0
    for lower in range(tree_level):
        initial_position = initial_position + level_counts[lower] * (4 - lower)
    return initial_position


def pair_ancestors(parent):
    sources, distances = pair_table()
    climbed = [jnp.arange(parent.shape[0], dtype=jnp.int32)]
    for distance in range(4):
        climbed.append(parent[climbed[-1]])
    return jnp.stack(
        [climbed[distance][source_node] for source_node, distance in zip(sources, distances)]
    )


def forward_products(panel_local, forward_stack, ancestor, pair_list, start_node, node_count):
    sources, distances = pair_table()
    chosen = np.array(pair_list, dtype=np.int32)
    feeders = np.array([sources[node_pairing] for node_pairing in pair_list], dtype=np.int32)
    products = jnp.einsum(
        "sjv,svk->sjk",
        panel_local[chosen],
        forward_stack[feeders],
        preferred_element_type=jnp.float32,
    )
    slots = jnp.arange(node_count, dtype=jnp.int32) + start_node
    onehot = (slots[:, None] == ancestor[chosen][None, :]).astype(jnp.float32)
    return jnp.einsum("kp,par->kar", onehot, products, precision=lax.Precision.HIGHEST)


def solve(right_side, diag_local, panel_local, ancestor):
    sources, distances = pair_table()
    node_total = right_side.shape[0]
    load_vector_count = right_side.shape[2]
    col_rows = diag_local.shape[1]
    leaf_rows = diag_local.shape[2]
    forward_stack = jnp.zeros((node_total, col_rows, load_vector_count), jnp.bfloat16)
    forward_levels = [None] * 5
    for tree_level in range(5):
        start_node = level_starts[tree_level]
        node_count = level_counts[tree_level]
        reduced = right_side[start_node : start_node + node_count]
        if tree_level > 0:
            arriving = [
                node_pairing
                for node_pairing in range(len(sources))
                if node_level(sources[node_pairing]) + distances[node_pairing] == tree_level
            ]
            partial_value = forward_products(
                panel_local, forward_stack, ancestor, arriving, start_node, node_count
            )
            reduced = reduced - lax.psum(partial_value.astype(jnp.bfloat16), "col").astype(
                jnp.float32
            )
        division_count = jnp.einsum(
            "kcl,klr->kcr",
            diag_local[start_node : start_node + node_count],
            reduced.astype(jnp.bfloat16),
            preferred_element_type=jnp.float32,
        )
        forward_value = lax.psum(division_count.astype(jnp.bfloat16), "leaf").astype(jnp.float32)
        forward_levels[tree_level] = forward_value
        forward_stack = forward_stack.at[start_node : start_node + node_count].set(
            forward_value.astype(jnp.bfloat16)
        )
    solution_stack = jnp.zeros((node_total, leaf_rows, load_vector_count), jnp.bfloat16)
    results = [None] * 5
    for tree_level in (4, 3, 2, 1, 0):
        start_node = level_starts[tree_level]
        node_count = level_counts[tree_level]
        corrected = forward_levels[tree_level]
        if tree_level < 4:
            initial_position = pair_offset(tree_level)
            span_pairs = node_count * (4 - tree_level)
            upper_node = solution_stack[ancestor[initial_position : initial_position + span_pairs]]
            products = jnp.einsum(
                "boj,boh->bjh",
                panel_local[initial_position : initial_position + span_pairs],
                upper_node,
                preferred_element_type=jnp.float32,
            )
            partial_value = jnp.sum(
                products.reshape(node_count, 4 - tree_level, col_rows, load_vector_count), axis=1
            )
            corrected = corrected - lax.psum(partial_value.astype(jnp.bfloat16), "leaf").astype(
                jnp.float32
            )
        division_count = jnp.einsum(
            "kcl,kcr->klr",
            diag_local[start_node : start_node + node_count],
            corrected.astype(jnp.bfloat16),
            preferred_element_type=jnp.float32,
        )
        solution = lax.psum(division_count.astype(jnp.bfloat16), "col").astype(jnp.float32)
        results[tree_level] = solution
        solution_stack = solution_stack.at[start_node : start_node + node_count].set(
            solution.astype(jnp.bfloat16)
        )
    return jnp.concatenate(results, axis=0)


def bf16(value):
    return value.astype(jnp.bfloat16)


def f32(value):
    return value.astype(jnp.float32)


def send(src, dst, sems, at, device):
    return pltpu.make_async_remote_copy(
        src_ref=src,
        dst_ref=dst,
        send_sem=sems[0].at[at],
        recv_sem=sems[1].at[at],
        device_id=device,
        device_id_type=MESH,
    )


class Leaf:
    def __init__(self, part, result, finish, half_in, first, first_in, second, second_in, sems):
        self.part, self.result, self.finish = part, result, finish
        self.half_in, self.first, self.first_in = half_in, first, first_in
        self.second, self.second_in, self.sems = second, second_in, sems
        me = lax.axis_index("leaf")
        self.core = me % 2
        self.sibling = {"leaf": me + 1 - 2 * self.core}
        self.along_x = {"leaf": me + 2 - 4 * ((me // 2) % 2)}
        self.along_y = {"leaf": me + 4 - 8 * (me // 4)}
        self.half = part.shape[1] // 2
        self.quarter = self.half // 2
        self.mine = pl.ds(self.core * self.half, self.half)
        self.other = pl.ds((1 - self.core) * self.half, self.half)

    def neighbours(self):
        return (self.sibling, self.along_x, self.along_y)

    def scatter(self, k):
        return send(self.part.at[k, self.other], self.half_in.at[k], self.sems[0], k, self.sibling)

    def exchange(self, k, step):
        source, target = ((self.first, self.first_in), (self.second, self.second_in))[step]
        low, high = pl.ds(0, self.quarter), pl.ds(self.quarter, self.quarter)
        ways = (self.along_x, self.along_y) if step == 0 else (self.along_y, self.along_x)
        return (
            send(source.at[k, low], target.at[k, low], self.sems[1 + 2 * step], k, ways[0]),
            send(source.at[k, high], target.at[k, high], self.sems[2 + 2 * step], k, ways[1]),
        )

    def gather(self, k):
        return send(self.result.at[k, self.mine], self.result.at[k, self.mine], self.sems[5], k, self.sibling)

    def stage_first(self, k):
        self.scatter(k).wait_recv()
        self.first[k] = bf16(f32(self.part[k, self.mine]) + f32(self.half_in[k]))
        for copy in self.exchange(k, 0):
            copy.start()

    def stage_second(self, k):
        for copy in self.exchange(k, 0):
            copy.wait_recv()
        self.second[k] = bf16(f32(self.first[k]) + f32(self.first_in[k]))
        for copy in self.exchange(k, 1):
            copy.start()

    def stage_result(self, k):
        for copy in self.exchange(k, 1):
            copy.wait_recv()
        total = f32(self.second[k]) + f32(self.second_in[k])
        self.result[k, self.mine] = self.finish(k, self.mine, total)
        self.gather(k).start()

    def stage_gathered(self, k):
        self.gather(k).wait_recv()

    def drain(self, k):
        self.scatter(k).wait_send()
        for copy in self.exchange(k, 0) + self.exchange(k, 1):
            copy.wait_send()
        self.gather(k).wait_send()


class Col:
    def __init__(self, part, result, arrived, joined, joined_in, sems):
        self.part, self.result, self.arrived = part, result, arrived
        self.joined, self.joined_in, self.sems = joined, joined_in, sems
        me = lax.axis_index("col")
        self.inner = jnp.logical_or(me == 1, me == 2)
        self.end = jnp.logical_or(me == 0, me == 3)
        self.end_partner = {"col": (me // 2) + 1}
        self.inner_partner = {"col": 3 - me}
        self.outer = {"col": (me // 2) * 3}

    def greet(self, barrier):
        @pl.when(self.end)
        def _():
            pl.semaphore_signal(barrier, inc=1, device_id=self.end_partner, device_id_type=MESH)

        @pl.when(self.inner)
        def _():
            pl.semaphore_signal(barrier, inc=1, device_id=self.inner_partner, device_id_type=MESH)
            pl.semaphore_signal(barrier, inc=1, device_id=self.outer, device_id_type=MESH)

    def to_inner(self, k):
        return send(self.part.at[k], self.arrived.at[k], self.sems[0], k, self.end_partner)

    def across(self, k):
        return send(self.joined.at[k], self.joined_in.at[k], self.sems[1], k, self.inner_partner)

    def to_end(self, k):
        return send(self.result.at[k], self.result.at[k], self.sems[2], k, self.outer)

    def stage_start(self, k):
        @pl.when(self.end)
        def _():
            self.to_inner(k).start()

    def stage_join(self, k):
        @pl.when(self.inner)
        def _():
            self.to_inner(k).wait_recv()
            self.joined[k] = bf16(f32(self.part[k]) + f32(self.arrived[k]))
            self.across(k).start()

    def stage_sum(self, k):
        @pl.when(self.inner)
        def _():
            self.across(k).wait_recv()
            self.result[k] = bf16(f32(self.joined[k]) + f32(self.joined_in[k]))
            self.to_end(k).start()

    def stage_end(self, k):
        @pl.when(self.end)
        def _():
            self.to_end(k).wait_recv()

    def drain(self, k):
        @pl.when(self.end)
        def _():
            self.to_inner(k).wait_send()

        @pl.when(self.inner)
        def _():
            self.across(k).wait_send()
            self.to_end(k).wait_send()


def enter(leaf, col):
    barrier = pltpu.get_barrier_semaphore()
    count = 0
    if leaf is not None:
        for neighbour in leaf.neighbours():
            pl.semaphore_signal(barrier, inc=1, device_id=neighbour, device_id_type=MESH)
        count = 3
    if col is None:
        pl.semaphore_wait(barrier, count)
    else:
        col.greet(barrier)

        @pl.when(col.end)
        def _():
            pl.semaphore_wait(barrier, count + 1)

        @pl.when(col.inner)
        def _():
            pl.semaphore_wait(barrier, count + 2)


def staged(count, stages):
    last = max(lag for lag, _ in stages)

    def body(step, carry):
        for lag, stage in reversed(stages):
            node = step - lag

            @pl.when(jnp.logical_and(node >= 0, node < count))
            def _(stage=stage, node=node):
                stage(node)

        return carry

    lax.fori_loop(0, count + last, body, 0)


def each(count, stage):
    def body(k, carry):
        stage(k)
        return carry

    lax.fori_loop(0, count, body, 0)


def pair_sems(refs, count):
    return [(refs[2 * at], refs[2 * at + 1]) for at in range(count)]


def forward_kernel(start, count, has_update, *refs):
    refs = list(refs)
    take = lambda number: [refs.pop(0) for _ in range(number)]
    update = take(1)[0] if has_update else None
    right_hbm, diag_hbm, y_ref, right, diag, load_sem = take(6)
    part, half_in, first, first_in, second, second_in = take(6)
    leaf_sems = pair_sems(take(12), 6)
    leaf = Leaf(
        part, y_ref, lambda k, rows, total: bf16(total), half_in, first, first_in, second, second_in, leaf_sems
    )
    col = None
    if has_update:
        summed, arrived, joined, joined_in = take(4)
        col = Col(update, summed, arrived, joined, joined_in, pair_sems(take(6), 3))
    units = count * SPLIT
    width = right.shape[3]
    loads = [
        pltpu.make_async_copy(
            right_hbm.at[pl.ds(start, count), :, pl.ds(half * width, width)], right.at[half], load_sem.at[half]
        )
        for half in range(SPLIT)
    ]
    loads.append(pltpu.make_async_copy(diag_hbm.at[pl.ds(start, count)], diag, load_sem.at[SPLIT]))
    for load in loads:
        load.start()
    enter(leaf, col)
    if has_update:
        each(units, col.stage_start)
    for load in loads:
        load.wait()

    def divide(k):
        reduced = right[k % SPLIT, k // SPLIT]
        if has_update:
            col.stage_end(k)
            reduced = reduced - f32(summed[k])
        part[k] = bf16(
            lax.dot_general(
                diag[k // SPLIT],
                bf16(reduced),
                (((0,), (0,)), ((), ())),
                preferred_element_type=jnp.float32,
            )
        )
        leaf.scatter(k).start()

    stages = []
    lag = 0
    if has_update:
        stages += [(0, col.stage_join), (LAG, col.stage_sum)]
        lag = LAG + 1
    stages += [
        (lag, divide),
        (lag + 1, leaf.stage_first),
        (lag + 1 + LAG, leaf.stage_second),
        (lag + 1 + 2 * LAG, leaf.stage_result),
    ]
    staged(units, stages)
    each(units, leaf.stage_gathered)
    each(units, leaf.drain)
    if has_update:
        each(units, col.drain)


def backward_kernel(start, count, has_update, *refs):
    refs = list(refs)
    take = lambda number: [refs.pop(0) for _ in range(number)]
    update = take(1)[0] if has_update else None
    y_ref, diag_hbm, x_ref, diag, load_sem, part, arrived, joined, joined_in = take(9)
    col = Col(part, x_ref, arrived, joined, joined_in, pair_sems(take(6), 3))
    leaf = None
    if has_update:
        z_ref, half_in, first, first_in, second, second_in = take(6)

        def finish(k, rows, total):
            return bf16(f32(y_ref[k, rows]) - total)

        leaf = Leaf(
            update, z_ref, finish, half_in, first, first_in, second, second_in, pair_sems(take(12), 6)
        )
    units = count * SPLIT
    load = pltpu.make_async_copy(diag_hbm.at[pl.ds(start, count)], diag, load_sem.at[0])
    load.start()
    enter(leaf, col)
    if has_update:
        each(units, lambda k: leaf.scatter(k).start())
    load.wait()

    def divide(k):
        if has_update:
            leaf.stage_gathered(k)
            corrected = z_ref[k]
        else:
            corrected = y_ref[k]
        part[k] = bf16(jnp.dot(diag[k // SPLIT], corrected, preferred_element_type=jnp.float32))
        col.stage_start(k)

    stages = []
    lag = 0
    if has_update:
        stages += [
            (0, leaf.stage_first),
            (LAG, leaf.stage_second),
            (2 * LAG, leaf.stage_result),
        ]
        lag = 2 * LAG + 1
    stages += [(lag, divide), (lag + LAG, col.stage_join), (lag + 2 * LAG, col.stage_sum)]
    staged(units, stages)
    each(units, col.stage_end)
    each(units, col.drain)
    if has_update:
        each(units, leaf.drain)


def leaf_scratch(units, rows, width):
    half = pltpu.VMEM((units, rows // 2, width), jnp.bfloat16)
    return [half] * 5


def sem_scratch(units, number):
    return [pltpu.SemaphoreType.DMA((units,))] * (2 * number)


def cost(flops, moved):
    return pl.CostEstimate(flops=flops, bytes_accessed=moved, transcendentals=0)


def forward_level(level, update, right_side, diag):
    start, count = level_starts[level], level_counts[level]
    depth, rows = diag.shape[1], diag.shape[2]
    rhs = right_side.shape[2]
    units, width = count * SPLIT, rhs // SPLIT
    has_update = update is not None
    block = pltpu.VMEM((units, depth, width), jnp.bfloat16)
    scratch = [
        pltpu.VMEM((SPLIT, count, depth, width), jnp.float32),
        pltpu.VMEM((count, depth, rows), jnp.bfloat16),
        pltpu.SemaphoreType.DMA((SPLIT + 1,)),
        pltpu.VMEM((units, rows, width), jnp.bfloat16),
    ]
    scratch += leaf_scratch(units, rows, width) + sem_scratch(units, 6)
    if has_update:
        scratch += [block] * 4 + sem_scratch(units, 3)
    vmem = pl.BlockSpec(memory_space=pltpu.VMEM)
    anywhere = pl.BlockSpec(memory_space=pl.ANY)
    return pl.pallas_call(
        functools.partial(forward_kernel, start, count, has_update),
        out_shape=jax.ShapeDtypeStruct((units, rows, width), jnp.bfloat16),
        in_specs=[vmem] * has_update + [anywhere] * 2,
        out_specs=vmem,
        scratch_shapes=scratch,
        name=f"forward_level_{level}",
        cost_estimate=cost(2 * count * rows * depth * rhs, 2 * count * rows * (depth + rhs)),
        compiler_params=pltpu.CompilerParams(
            collective_id=level, has_side_effects=True, vmem_limit_bytes=VMEM_BYTES
        ),
    )(*([update] * has_update), right_side, diag)


def backward_level(level, update, forward_value, diag):
    start, count = level_starts[level], level_counts[level]
    depth, rows = diag.shape[1], diag.shape[2]
    units, width = forward_value.shape[0], forward_value.shape[2]
    has_update = update is not None
    block = pltpu.VMEM((units, depth, width), jnp.bfloat16)
    scratch = [pltpu.VMEM((count, depth, rows), jnp.bfloat16), pltpu.SemaphoreType.DMA((1,))]
    scratch += [block] * 4 + sem_scratch(units, 3)
    if has_update:
        scratch += [pltpu.VMEM((units, rows, width), jnp.bfloat16)]
        scratch += leaf_scratch(units, rows, width) + sem_scratch(units, 6)
    vmem = pl.BlockSpec(memory_space=pltpu.VMEM)
    anywhere = pl.BlockSpec(memory_space=pl.ANY)
    return pl.pallas_call(
        functools.partial(backward_kernel, start, count, has_update),
        out_shape=jax.ShapeDtypeStruct((units, depth, width), jnp.bfloat16),
        in_specs=[vmem] * has_update + [vmem, anywhere],
        out_specs=vmem,
        scratch_shapes=scratch,
        name=f"backward_level_{level}",
        cost_estimate=cost(2 * units * rows * depth * width, 2 * count * rows * depth),
        compiler_params=pltpu.CompilerParams(
            collective_id=5 + level, has_side_effects=True, vmem_limit_bytes=VMEM_BYTES
        ),
    )(*([update] * has_update), forward_value, diag)


def climb(parent_ref, node, distance):
    for _ in range(distance):
        node = parent_ref[node]
    return node


def joined_columns(ref):
    return jnp.concatenate([ref[half] for half in range(SPLIT)], axis=1)


def forward_update(level, panels, value, earlier, parent):
    count, start = level_counts[level], level_starts[level]
    rows, depth = panels.shape[1], panels.shape[2]
    width = value.shape[2]
    rhs = width * SPLIT
    distances = 4 - level
    base = pair_offset(level)
    above = level_counts[level + 1 :]
    given = len(earlier)

    def body(parent_ref, *refs):
        panel, values, before = refs[:distances], refs[distances], refs[distances + 1 : distances + 1 + given]
        done, beyond, total = refs[distances + 1 + given], refs[distances + 2 + given : -1], refs[-1]
        sums = (total, *beyond)
        k = pl.program_id(0)

        @pl.when(k == 0)
        def _():
            for at in range(distances):
                sums[at][...] = before[at][...] if given else jnp.zeros_like(sums[at])

        known = joined_columns(values)
        node = start + k
        for at in range(distances):
            node = parent_ref[node]
            slot = node - level_starts[level + 1 + at]
            sums[at][slot] += jnp.dot(panel[at][0], known, preferred_element_type=jnp.float32)

        @pl.when(k == count - 1)
        def _():
            for slot in range(above[0]):
                for half in range(SPLIT):
                    done[slot * SPLIT + half] = bf16(total[slot, :, half * width : (half + 1) * width])

    def panel_at(d):
        return lambda k, parent_ref: (base + k * distances + d, 0, 0)

    whole = lambda shape: pl.BlockSpec(shape, lambda k, parent_ref: (0, 0, 0))
    shapes = [(number, rows, rhs) for number in above]
    outs = pl.pallas_call(
        body,
        grid_spec=pltpu.PrefetchScalarGridSpec(
            num_scalar_prefetch=1,
            grid=(count,),
            in_specs=[pl.BlockSpec((1, rows, depth), panel_at(d)) for d in range(distances)]
            + [pl.BlockSpec((SPLIT, depth, width), lambda k, parent_ref: (k, 0, 0))]
            + [whole(shape) for shape in shapes[: given]],
            out_specs=[whole((above[0] * SPLIT, rows, width))] + [whole(shape) for shape in shapes[1:]],
            scratch_shapes=[pltpu.VMEM(shapes[0], jnp.float32)],
        ),
        out_shape=[jax.ShapeDtypeStruct((above[0] * SPLIT, rows, width), jnp.bfloat16)]
        + [jax.ShapeDtypeStruct(shape, jnp.float32) for shape in shapes[1:]],
        name=f"forward_update_{level}",
        cost_estimate=cost(
            2 * count * distances * rows * depth * rhs, 2 * count * depth * (distances * rows + rhs)
        ),
        compiler_params=pltpu.CompilerParams(vmem_limit_bytes=VMEM_BYTES),
    )(parent, *([panels] * distances), value, *earlier)
    return outs[0], outs[1:]


def backward_update(level, panels, solutions, parent):
    count, start = level_counts[level], level_starts[level]
    rows, depth = panels.shape[1], panels.shape[2]
    width = solutions[4].shape[2]
    distances = 4 - level
    base = pair_offset(level)

    def body(parent_ref, *refs):
        total = None
        for d in range(distances):
            product = lax.dot_general(
                refs[d][0],
                joined_columns(refs[distances + d]),
                (((0,), (0,)), ((), ())),
                preferred_element_type=jnp.float32,
            )
            total = product if total is None else total + product
        for half in range(SPLIT):
            refs[2 * distances][half] = bf16(total[:, half * width : (half + 1) * width])

    def panel_at(d):
        return lambda k, parent_ref: (base + k * distances + d, 0, 0)

    def upper_at(d):
        first = level_starts[level + 1 + d]
        return lambda k, parent_ref: (climb(parent_ref, start + k, d + 1) - first, 0, 0)

    return pl.pallas_call(
        body,
        grid_spec=pltpu.PrefetchScalarGridSpec(
            num_scalar_prefetch=1,
            grid=(count,),
            in_specs=[pl.BlockSpec((1, rows, depth), panel_at(d)) for d in range(distances)]
            + [pl.BlockSpec((SPLIT, rows, width), upper_at(d)) for d in range(distances)],
            out_specs=pl.BlockSpec((SPLIT, depth, width), lambda k, _: (k, 0, 0)),
        ),
        out_shape=jax.ShapeDtypeStruct((count * SPLIT, depth, width), jnp.bfloat16),
        name=f"backward_update_{level}",
        cost_estimate=cost(
            2 * count * distances * rows * depth * width * SPLIT, 2 * count * distances * rows * depth
        ),
        compiler_params=pltpu.CompilerParams(vmem_limit_bytes=VMEM_BYTES),
    )(parent, *([panels] * distances), *[solutions[level + 1 + d] for d in range(distances)])


def assemble(solutions, node_total):
    rows, width = solutions[0].shape[1], solutions[0].shape[2]

    def body(*refs):
        out = refs[5]
        for level in range(5):

            def store(k, level=level):
                for half in range(SPLIT):
                    out[level_starts[level] + k, :, half * width : (half + 1) * width] = f32(
                        refs[level][k * SPLIT + half]
                    )

            each(level_counts[level], store)

    return pl.pallas_call(
        body,
        out_shape=jax.ShapeDtypeStruct((node_total, rows, width * SPLIT), jnp.float32),
        in_specs=[pl.BlockSpec(memory_space=pltpu.VMEM)] * 5,
        out_specs=pl.BlockSpec(memory_space=pltpu.VMEM),
        name="assemble",
        cost_estimate=cost(0, node_total * rows * width * SPLIT * 6),
        compiler_params=pltpu.CompilerParams(vmem_limit_bytes=VMEM_BYTES),
    )(*solutions)


def shards(right_side, reciprocal_pivot_matrix, panels, parent):
    diag = jnp.swapaxes(reciprocal_pivot_matrix, 1, 2)
    values = [forward_level(0, None, right_side, diag)]
    earlier = ()
    for level in range(4):
        update, earlier = forward_update(level, panels, values[level], earlier, parent)
        values.append(forward_level(level + 1, update, right_side, diag))
    solutions = [None] * 5
    for level in (4, 3, 2, 1, 0):
        update = backward_update(level, panels, solutions, parent) if level < 4 else None
        solutions[level] = backward_level(level, update, values[level], diag)
    return assemble(solutions, right_side.shape[0])


def shards_any(right_side, reciprocal_pivot_matrix, panels, parent):
    ancestor = pair_ancestors(parent)
    return solve(right_side, reciprocal_pivot_matrix, panels, ancestor)


def solution(mesh):
    kernels = mesh.shape["leaf"] == 8 and mesh.shape["col"] == 4
    return jax.shard_map(
        shards if kernels else shards_any,
        mesh=mesh,
        in_specs=(P(None, "leaf", None), P(None, "col", "leaf"), P(None, "leaf", "col"), P()),
        out_specs=P(None, "leaf", None),
        check_vma=False,
    )
```

```python
import functools

import jax
import jax.numpy as jnp
import numpy as np
from jax import lax
from jax.experimental import pallas as pl
from jax.experimental.pallas import tpu as pltpu
from jax.sharding import PartitionSpec as P

MESH = pl.DeviceIdType.MESH
VMEM_BYTES = 58 * 2**20
LAG = 2
SPLITS = (1, 2, 2, 2, 2)


level_starts = (0, 16, 24, 28, 30)
level_counts = (16, 8, 4, 2, 1)


def pair_table():
    sources = []
    distances = []
    for tree_level in range(5):
        for tree_vertex in range(
            level_starts[tree_level], level_starts[tree_level] + level_counts[tree_level]
        ):
            for distance in range(1, 5 - tree_level):
                sources.append(tree_vertex)
                distances.append(distance)
    return (sources, distances)


def node_level(tree_vertex):
    deepest = 0
    for tree_level in range(5):
        if level_starts[tree_level] <= tree_vertex:
            deepest = tree_level
    return deepest


def pair_offset(tree_level):
    initial_position = 0
    for lower in range(tree_level):
        initial_position = initial_position + level_counts[lower] * (4 - lower)
    return initial_position


def pair_ancestors(parent):
    sources, distances = pair_table()
    climbed = [jnp.arange(parent.shape[0], dtype=jnp.int32)]
    for distance in range(4):
        climbed.append(parent[climbed[-1]])
    return jnp.stack(
        [climbed[distance][source_node] for source_node, distance in zip(sources, distances)]
    )


def forward_products(panel_local, forward_stack, ancestor, pair_list, start_node, node_count):
    sources, distances = pair_table()
    chosen = np.array(pair_list, dtype=np.int32)
    feeders = np.array([sources[node_pairing] for node_pairing in pair_list], dtype=np.int32)
    products = jnp.einsum(
        "sjv,svk->sjk",
        panel_local[chosen],
        forward_stack[feeders],
        preferred_element_type=jnp.float32,
    )
    slots = jnp.arange(node_count, dtype=jnp.int32) + start_node
    onehot = (slots[:, None] == ancestor[chosen][None, :]).astype(jnp.float32)
    return jnp.einsum("kp,par->kar", onehot, products, precision=lax.Precision.HIGHEST)


def solve(right_side, diag_local, panel_local, ancestor):
    sources, distances = pair_table()
    node_total = right_side.shape[0]
    load_vector_count = right_side.shape[2]
    col_rows = diag_local.shape[1]
    leaf_rows = diag_local.shape[2]
    forward_stack = jnp.zeros((node_total, col_rows, load_vector_count), jnp.bfloat16)
    forward_levels = [None] * 5
    for tree_level in range(5):
        start_node = level_starts[tree_level]
        node_count = level_counts[tree_level]
        reduced = right_side[start_node : start_node + node_count]
        if tree_level > 0:
            arriving = [
                node_pairing
                for node_pairing in range(len(sources))
                if node_level(sources[node_pairing]) + distances[node_pairing] == tree_level
            ]
            partial_value = forward_products(
                panel_local, forward_stack, ancestor, arriving, start_node, node_count
            )
            reduced = reduced - lax.psum(partial_value.astype(jnp.bfloat16), "col").astype(
                jnp.float32
            )
        division_count = jnp.einsum(
            "kcl,klr->kcr",
            diag_local[start_node : start_node + node_count],
            reduced.astype(jnp.bfloat16),
            preferred_element_type=jnp.float32,
        )
        forward_value = lax.psum(division_count.astype(jnp.bfloat16), "leaf").astype(jnp.float32)
        forward_levels[tree_level] = forward_value
        forward_stack = forward_stack.at[start_node : start_node + node_count].set(
            forward_value.astype(jnp.bfloat16)
        )
    solution_stack = jnp.zeros((node_total, leaf_rows, load_vector_count), jnp.bfloat16)
    results = [None] * 5
    for tree_level in (4, 3, 2, 1, 0):
        start_node = level_starts[tree_level]
        node_count = level_counts[tree_level]
        corrected = forward_levels[tree_level]
        if tree_level < 4:
            initial_position = pair_offset(tree_level)
            span_pairs = node_count * (4 - tree_level)
            upper_node = solution_stack[ancestor[initial_position : initial_position + span_pairs]]
            products = jnp.einsum(
                "boj,boh->bjh",
                panel_local[initial_position : initial_position + span_pairs],
                upper_node,
                preferred_element_type=jnp.float32,
            )
            partial_value = jnp.sum(
                products.reshape(node_count, 4 - tree_level, col_rows, load_vector_count), axis=1
            )
            corrected = corrected - lax.psum(partial_value.astype(jnp.bfloat16), "leaf").astype(
                jnp.float32
            )
        division_count = jnp.einsum(
            "kcl,kcr->klr",
            diag_local[start_node : start_node + node_count],
            corrected.astype(jnp.bfloat16),
            preferred_element_type=jnp.float32,
        )
        solution = lax.psum(division_count.astype(jnp.bfloat16), "col").astype(jnp.float32)
        results[tree_level] = solution
        solution_stack = solution_stack.at[start_node : start_node + node_count].set(
            solution.astype(jnp.bfloat16)
        )
    return jnp.concatenate(results, axis=0)


def bf16(value):
    return value.astype(jnp.bfloat16)


def f32(value):
    return value.astype(jnp.float32)


def send(src, dst, sems, at, device):
    return pltpu.make_async_remote_copy(
        src_ref=src,
        dst_ref=dst,
        send_sem=sems[0].at[at],
        recv_sem=sems[1].at[at],
        device_id=device,
        device_id_type=MESH,
    )


class Leaf:
    def __init__(self, part, result, finish, half_in, first, first_in, second, second_in, sems):
        self.part, self.result, self.finish = part, result, finish
        self.half_in, self.first, self.first_in = half_in, first, first_in
        self.second, self.second_in, self.sems = second, second_in, sems
        me = lax.axis_index("leaf")
        self.core = me % 2
        self.sibling = {"leaf": me + 1 - 2 * self.core}
        self.along_x = {"leaf": me + 2 - 4 * ((me // 2) % 2)}
        self.along_y = {"leaf": me + 4 - 8 * (me // 4)}
        self.half = part.shape[1] // 2
        self.quarter = self.half // 2
        self.mine = pl.ds(self.core * self.half, self.half)
        self.other = pl.ds((1 - self.core) * self.half, self.half)

    def neighbours(self):
        return (self.sibling, self.along_x, self.along_y)

    def scatter(self, k):
        return send(self.part.at[k, self.other], self.half_in.at[k], self.sems[0], k, self.sibling)

    def exchange(self, k, step):
        source, target = ((self.first, self.first_in), (self.second, self.second_in))[step]
        low, high = pl.ds(0, self.quarter), pl.ds(self.quarter, self.quarter)
        ways = (self.along_x, self.along_y) if step == 0 else (self.along_y, self.along_x)
        return (
            send(source.at[k, low], target.at[k, low], self.sems[1 + 2 * step], k, ways[0]),
            send(source.at[k, high], target.at[k, high], self.sems[2 + 2 * step], k, ways[1]),
        )

    def gather(self, k):
        return send(self.result.at[k, self.mine], self.result.at[k, self.mine], self.sems[5], k, self.sibling)

    def stage_first(self, k):
        self.scatter(k).wait_recv()
        self.first[k] = bf16(f32(self.part[k, self.mine]) + f32(self.half_in[k]))
        for copy in self.exchange(k, 0):
            copy.start()

    def stage_second(self, k):
        for copy in self.exchange(k, 0):
            copy.wait_recv()
        self.second[k] = bf16(f32(self.first[k]) + f32(self.first_in[k]))
        for copy in self.exchange(k, 1):
            copy.start()

    def stage_result(self, k):
        for copy in self.exchange(k, 1):
            copy.wait_recv()
        total = f32(self.second[k]) + f32(self.second_in[k])
        self.result[k, self.mine] = self.finish(k, self.mine, total)
        self.gather(k).start()

    def stage_gathered(self, k):
        self.gather(k).wait_recv()

    def drain(self, k):
        self.scatter(k).wait_send()
        for copy in self.exchange(k, 0) + self.exchange(k, 1):
            copy.wait_send()
        self.gather(k).wait_send()


class Col:
    def __init__(self, part, result, arrived, joined, joined_in, sems):
        self.part, self.result, self.arrived = part, result, arrived
        self.joined, self.joined_in, self.sems = joined, joined_in, sems
        me = lax.axis_index("col")
        self.inner = jnp.logical_or(me == 1, me == 2)
        self.end = jnp.logical_or(me == 0, me == 3)
        self.end_partner = {"col": (me // 2) + 1}
        self.inner_partner = {"col": 3 - me}
        self.outer = {"col": (me // 2) * 3}

    def greet(self, barrier):
        @pl.when(self.end)
        def _():
            pl.semaphore_signal(barrier, inc=1, device_id=self.end_partner, device_id_type=MESH)

        @pl.when(self.inner)
        def _():
            pl.semaphore_signal(barrier, inc=1, device_id=self.inner_partner, device_id_type=MESH)
            pl.semaphore_signal(barrier, inc=1, device_id=self.outer, device_id_type=MESH)

    def to_inner(self, k):
        return send(self.part.at[k], self.arrived.at[k], self.sems[0], k, self.end_partner)

    def across(self, k):
        return send(self.joined.at[k], self.joined_in.at[k], self.sems[1], k, self.inner_partner)

    def to_end(self, k):
        return send(self.result.at[k], self.result.at[k], self.sems[2], k, self.outer)

    def stage_start(self, k):
        @pl.when(self.end)
        def _():
            self.to_inner(k).start()

    def stage_join(self, k):
        @pl.when(self.inner)
        def _():
            self.to_inner(k).wait_recv()
            self.joined[k] = bf16(f32(self.part[k]) + f32(self.arrived[k]))
            self.across(k).start()

    def stage_sum(self, k):
        @pl.when(self.inner)
        def _():
            self.across(k).wait_recv()
            self.result[k] = bf16(f32(self.joined[k]) + f32(self.joined_in[k]))
            self.to_end(k).start()

    def stage_end(self, k):
        @pl.when(self.end)
        def _():
            self.to_end(k).wait_recv()

    def drain(self, k):
        @pl.when(self.end)
        def _():
            self.to_inner(k).wait_send()

        @pl.when(self.inner)
        def _():
            self.across(k).wait_send()
            self.to_end(k).wait_send()


def enter(leaf, col):
    barrier = pltpu.get_barrier_semaphore()
    count = 0
    if leaf is not None:
        for neighbour in leaf.neighbours():
            pl.semaphore_signal(barrier, inc=1, device_id=neighbour, device_id_type=MESH)
        count = 3
    if col is None:
        pl.semaphore_wait(barrier, count)
    else:
        col.greet(barrier)

        @pl.when(col.end)
        def _():
            pl.semaphore_wait(barrier, count + 1)

        @pl.when(col.inner)
        def _():
            pl.semaphore_wait(barrier, count + 2)


def staged(count, stages):
    last = max(lag for lag, _ in stages)

    def body(step, carry):
        for lag, stage in reversed(stages):
            node = step - lag

            @pl.when(jnp.logical_and(node >= 0, node < count))
            def _(stage=stage, node=node):
                stage(node)

        return carry

    lax.fori_loop(0, count + last, body, 0)


def each(count, stage):
    def body(k, carry):
        stage(k)
        return carry

    lax.fori_loop(0, count, body, 0)


def pair_sems(refs, count):
    return [(refs[2 * at], refs[2 * at + 1]) for at in range(count)]


def forward_kernel(start, count, has_update, *refs):
    refs = list(refs)
    take = lambda number: [refs.pop(0) for _ in range(number)]
    update = take(1)[0] if has_update else None
    right_hbm, diag_hbm, y_ref, right, diag, load_sem = take(6)
    part, half_in, first, first_in, second, second_in = take(6)
    leaf_sems = pair_sems(take(12), 6)
    leaf = Leaf(
        part, y_ref, lambda k, rows, total: bf16(total), half_in, first, first_in, second, second_in, leaf_sems
    )
    col = None
    if has_update:
        summed, arrived, joined, joined_in = take(4)
        col = Col(update, summed, arrived, joined, joined_in, pair_sems(take(6), 3))
    split, width = right.shape[0], right.shape[3]
    units = count * split
    loads = [
        pltpu.make_async_copy(
            right_hbm.at[pl.ds(start, count), :, pl.ds(half * width, width)], right.at[half], load_sem.at[half]
        )
        for half in range(split)
    ]
    loads.append(pltpu.make_async_copy(diag_hbm.at[pl.ds(start, count)], diag, load_sem.at[split]))
    for load in loads:
        load.start()
    enter(leaf, col)
    if has_update:
        each(units, col.stage_start)
    for load in loads:
        load.wait()

    def divide(k):
        reduced = right[k % split, k // split]
        if has_update:
            col.stage_end(k)
            reduced = reduced - f32(summed[k])
        part[k] = bf16(
            lax.dot_general(
                diag[k // split],
                bf16(reduced),
                (((0,), (0,)), ((), ())),
                preferred_element_type=jnp.float32,
            )
        )
        leaf.scatter(k).start()

    stages = []
    lag = 0
    if has_update:
        stages += [(0, col.stage_join), (LAG, col.stage_sum)]
        lag = LAG + 1
    stages += [
        (lag, divide),
        (lag + 1, leaf.stage_first),
        (lag + 1 + LAG, leaf.stage_second),
        (lag + 1 + 2 * LAG, leaf.stage_result),
    ]

    def finish(k):
        leaf.stage_gathered(k)
        leaf.drain(k)
        if has_update:
            col.drain(k)

    stages.append((lag + 1 + 3 * LAG, finish))
    staged(units, stages)


def backward_kernel(start, count, units, has_update, lower, uppers, *refs):
    refs = list(refs)
    take = lambda number: [refs.pop(0) for _ in range(number)]
    update = take(1)[0] if has_update else None
    y_ref, diag_hbm = take(2)
    if lower is not None:
        parent_ref, panels_hbm = take(2)
        known = take(len(uppers))
    x_ref = take(1)[0]
    if lower is not None:
        partial_ref = take(1)[0]
    diag, load_sem, part, arrived, joined, joined_in = take(6)
    col = Col(part, x_ref, arrived, joined, joined_in, pair_sems(take(6), 3))
    leaf = None
    if has_update:
        z_ref, half_in, first, first_in, second, second_in = take(6)

        def corrected_half(k, rows, total):
            return bf16(f32(y_ref[k, rows]) - total)

        leaf = Leaf(
            update, z_ref, corrected_half, half_in, first, first_in, second, second_in, pair_sems(take(12), 6)
        )
    if lower is not None:
        panel, panel_sem = take(2)
        distances = 4 - lower

        def fetch(k):
            at = pair_offset(lower) + k * distances + 1
            return pltpu.make_async_copy(
                panels_hbm.at[pl.ds(at, distances - 1)], panel.at[k % 2], panel_sem.at[k % 2]
            )

        for k in range(2):
            fetch(k).start()

    def extra(k):
        fetch(k).wait()
        node = parent_ref[level_starts[lower] + k]
        total = None
        for at, upper in enumerate(uppers):
            node = parent_ref[node]
            split = SPLITS[upper]
            slot = jnp.clip(node - level_starts[upper], 0, level_counts[upper] - 1) * split
            value = jnp.concatenate([known[at][slot + half] for half in range(split)], axis=1)
            product = lax.dot_general(
                panel[k % 2, at], value, (((0,), (0,)), ((), ())), preferred_element_type=jnp.float32
            )
            total = product if total is None else total + product
        partial_ref[k] = bf16(total)

        @pl.when(k + 2 < level_counts[lower])
        def _():
            fetch(k + 2).start()

    split = units // count
    load = pltpu.make_async_copy(diag_hbm.at[pl.ds(start, count)], diag, load_sem.at[0])
    load.start()
    enter(leaf, col)
    if has_update:
        each(units, lambda k: leaf.scatter(k).start())
    load.wait()

    def divide(k):
        if has_update:
            leaf.stage_gathered(k)
            corrected = z_ref[k]
        else:
            corrected = y_ref[k]
        part[k] = bf16(jnp.dot(diag[k // split], corrected, preferred_element_type=jnp.float32))
        col.stage_start(k)

    stages = []
    lag = 0
    if has_update:
        stages += [
            (0, leaf.stage_first),
            (LAG, leaf.stage_second),
            (2 * LAG, leaf.stage_result),
        ]
        lag = 2 * LAG + 1
    stages += [(lag, divide), (lag + LAG, col.stage_join), (lag + 2 * LAG, col.stage_sum)]

    def finish(k):
        col.stage_end(k)
        col.drain(k)
        if has_update:
            leaf.drain(k)

    stages.append((lag + 3 * LAG, finish))
    if lower is not None:
        stages.insert(0, (1, extra))
    staged(units, stages)


def leaf_scratch(units, rows, width):
    half = pltpu.VMEM((units, rows // 2, width), jnp.bfloat16)
    return [half] * 5


def sem_scratch(units, number):
    return [pltpu.SemaphoreType.DMA((units,))] * (2 * number)


def cost(flops, moved):
    return pl.CostEstimate(flops=flops, bytes_accessed=moved, transcendentals=0)


def forward_level(level, update, right_side, diag):
    start, count = level_starts[level], level_counts[level]
    depth, rows = diag.shape[1], diag.shape[2]
    rhs = right_side.shape[2]
    split = SPLITS[level]
    units, width = count * split, rhs // split
    has_update = update is not None
    block = pltpu.VMEM((units, depth, width), jnp.bfloat16)
    scratch = [
        pltpu.VMEM((split, count, depth, width), jnp.float32),
        pltpu.VMEM((count, depth, rows), jnp.bfloat16),
        pltpu.SemaphoreType.DMA((split + 1,)),
        pltpu.VMEM((units, rows, width), jnp.bfloat16),
    ]
    scratch += leaf_scratch(units, rows, width) + sem_scratch(units, 6)
    if has_update:
        scratch += [block] * 4 + sem_scratch(units, 3)
    vmem = pl.BlockSpec(memory_space=pltpu.VMEM)
    anywhere = pl.BlockSpec(memory_space=pl.ANY)
    return pl.pallas_call(
        functools.partial(forward_kernel, start, count, has_update),
        out_shape=jax.ShapeDtypeStruct((units, rows, width), jnp.bfloat16),
        in_specs=[vmem] * has_update + [anywhere] * 2,
        out_specs=vmem,
        scratch_shapes=scratch,
        name=f"forward_level_{level}",
        cost_estimate=cost(2 * count * rows * depth * rhs, 2 * count * rows * (depth + rhs)),
        compiler_params=pltpu.CompilerParams(
            collective_id=level, has_side_effects=True, vmem_limit_bytes=VMEM_BYTES
        ),
    )(*([update] * has_update), right_side, diag)


def backward_level(level, update, forward_value, diag, panels, solutions, parent):
    start, count = level_starts[level], level_counts[level]
    depth, rows = diag.shape[1], diag.shape[2]
    units, width = forward_value.shape[0], forward_value.shape[2]
    has_update = update is not None
    block = pltpu.VMEM((units, depth, width), jnp.bfloat16)
    scratch = [pltpu.VMEM((count, depth, rows), jnp.bfloat16), pltpu.SemaphoreType.DMA((1,))]
    scratch += [block] * 4 + sem_scratch(units, 3)
    if has_update:
        scratch += [pltpu.VMEM((units, rows, width), jnp.bfloat16)]
        scratch += leaf_scratch(units, rows, width) + sem_scratch(units, 6)
    vmem = pl.BlockSpec(memory_space=pltpu.VMEM)
    anywhere = pl.BlockSpec(memory_space=pl.ANY)
    lower = level - 1 if 1 <= level <= 3 else None
    uppers = list(range(level + 1, 5)) if lower is not None else []
    out_shape = [jax.ShapeDtypeStruct((units, depth, width), jnp.bfloat16)]
    extra_specs, extra_args = [], []
    if lower is not None:
        rhs = width * SPLITS[level]
        out_shape.append(jax.ShapeDtypeStruct((level_counts[lower], rows, rhs), jnp.bfloat16))
        extra_specs = [pl.BlockSpec(memory_space=pltpu.SMEM), anywhere] + [vmem] * len(uppers)
        extra_args = [parent, panels] + [solutions[upper] for upper in uppers]
        scratch += [
            pltpu.VMEM((2, 3 - lower, depth, rows), jnp.bfloat16),
            pltpu.SemaphoreType.DMA((2,)),
        ]
    outs = pl.pallas_call(
        functools.partial(backward_kernel, start, count, units, has_update, lower, uppers),
        out_shape=out_shape,
        in_specs=[vmem] * has_update + [vmem, anywhere] + extra_specs,
        out_specs=[vmem] * len(out_shape),
        scratch_shapes=scratch,
        name=f"backward_level_{level}",
        cost_estimate=cost(2 * units * rows * depth * width, 2 * count * rows * depth),
        compiler_params=pltpu.CompilerParams(
            collective_id=5 + level, has_side_effects=True, vmem_limit_bytes=VMEM_BYTES
        ),
    )(*([update] * has_update), forward_value, diag, *extra_args)
    return outs[0], (outs[1] if lower is not None else None)


def joined_columns(ref):
    return jnp.concatenate([ref[half] for half in range(ref.shape[0])], axis=1)


def forward_update(level, panels, value, earlier, parent):
    count, start = level_counts[level], level_starts[level]
    rows, depth = panels.shape[1], panels.shape[2]
    own, split = SPLITS[level], SPLITS[level + 1]
    rhs = value.shape[2] * own
    width = rhs // split
    distances = 4 - level
    base = pair_offset(level)
    above = level_counts[level + 1 :]
    given = len(earlier)

    def body(parent_ref, *refs):
        panel, values, before = refs[:distances], refs[distances], refs[distances + 1 : distances + 1 + given]
        done, beyond, total = refs[distances + 1 + given], refs[distances + 2 + given : -1], refs[-1]
        sums = (total, *beyond)
        k = pl.program_id(0)

        @pl.when(k == 0)
        def _():
            for at in range(distances):
                sums[at][...] = before[at][...] if given else jnp.zeros_like(sums[at])

        known = joined_columns(values)
        node = start + k
        for at in range(distances):
            node = parent_ref[node]
            slot = node - level_starts[level + 1 + at]
            sums[at][slot] += jnp.dot(panel[at][0], known, preferred_element_type=jnp.float32)

        @pl.when(k == count - 1)
        def _():
            for slot in range(above[0]):
                for half in range(split):
                    done[slot * split + half] = bf16(total[slot, :, half * width : (half + 1) * width])

    def panel_at(d):
        return lambda k, parent_ref: (base + k * distances + d, 0, 0)

    whole = lambda shape: pl.BlockSpec(shape, lambda k, parent_ref: (0, 0, 0))
    shapes = [(number, rows, rhs) for number in above]
    outs = pl.pallas_call(
        body,
        grid_spec=pltpu.PrefetchScalarGridSpec(
            num_scalar_prefetch=1,
            grid=(count,),
            in_specs=[pl.BlockSpec((1, rows, depth), panel_at(d)) for d in range(distances)]
            + [pl.BlockSpec((own, depth, rhs // own), lambda k, parent_ref: (k, 0, 0))]
            + [whole(shape) for shape in shapes[: given]],
            out_specs=[whole((above[0] * split, rows, width))] + [whole(shape) for shape in shapes[1:]],
            scratch_shapes=[pltpu.VMEM(shapes[0], jnp.float32)],
        ),
        out_shape=[jax.ShapeDtypeStruct((above[0] * split, rows, width), jnp.bfloat16)]
        + [jax.ShapeDtypeStruct(shape, jnp.float32) for shape in shapes[1:]],
        name=f"forward_update_{level}",
        cost_estimate=cost(
            2 * count * distances * rows * depth * rhs, 2 * count * depth * (distances * rows + rhs)
        ),
        compiler_params=pltpu.CompilerParams(vmem_limit_bytes=VMEM_BYTES),
    )(parent, *([panels] * distances), value, *earlier)
    return outs[0], outs[1:]


def backward_update(level, panels, solutions, partial, parent):
    count, start = level_counts[level], level_starts[level]
    rows, depth = panels.shape[1], panels.shape[2]
    own, split = SPLITS[level + 1], SPLITS[level]
    rhs = solutions[level + 1].shape[2] * own
    width = rhs // split
    distances = 4 - level
    base = pair_offset(level)
    first = level_starts[level + 1]
    given = partial is not None

    def body(parent_ref, panel, upper, *refs):
        total = lax.dot_general(
            panel[0], joined_columns(upper), (((0,), (0,)), ((), ())), preferred_element_type=jnp.float32
        )
        if given:
            total = total + f32(refs[0][0])
        for half in range(split):
            refs[-1][half] = bf16(total[:, half * width : (half + 1) * width])

    return pl.pallas_call(
        body,
        grid_spec=pltpu.PrefetchScalarGridSpec(
            num_scalar_prefetch=1,
            grid=(count,),
            in_specs=[
                pl.BlockSpec((1, rows, depth), lambda k, parent_ref: (base + k * distances, 0, 0)),
                pl.BlockSpec(
                    (own, rows, rhs // own), lambda k, parent_ref: (parent_ref[start + k] - first, 0, 0)
                ),
            ]
            + [pl.BlockSpec((1, depth, rhs), lambda k, parent_ref: (k, 0, 0))] * given,
            out_specs=pl.BlockSpec((split, depth, width), lambda k, parent_ref: (k, 0, 0)),
        ),
        out_shape=jax.ShapeDtypeStruct((count * split, depth, width), jnp.bfloat16),
        name=f"backward_update_{level}",
        cost_estimate=cost(2 * count * rows * depth * rhs, 2 * count * rows * depth),
        compiler_params=pltpu.CompilerParams(vmem_limit_bytes=VMEM_BYTES),
    )(parent, panels, solutions[level + 1], *([partial] * given))


def assemble(solutions, node_total):
    rows = solutions[0].shape[1]
    rhs = solutions[0].shape[2] * SPLITS[0]

    def body(*refs):
        out = refs[5]
        for level in range(5):

            def store(k, level=level):
                split = SPLITS[level]
                width = rhs // split
                for half in range(split):
                    out[level_starts[level] + k, :, half * width : (half + 1) * width] = f32(
                        refs[level][k * split + half]
                    )

            each(level_counts[level], store)

    return pl.pallas_call(
        body,
        out_shape=jax.ShapeDtypeStruct((node_total, rows, rhs), jnp.float32),
        in_specs=[pl.BlockSpec(memory_space=pltpu.VMEM)] * 5,
        out_specs=pl.BlockSpec(memory_space=pltpu.VMEM),
        name="assemble",
        cost_estimate=cost(0, node_total * rows * rhs * 6),
        compiler_params=pltpu.CompilerParams(vmem_limit_bytes=VMEM_BYTES),
    )(*solutions)


def shards(right_side, reciprocal_pivot_matrix, panels, parent):
    diag = jnp.swapaxes(reciprocal_pivot_matrix, 1, 2)
    values = [forward_level(0, None, right_side, diag)]
    earlier = ()
    for level in range(4):
        update, earlier = forward_update(level, panels, values[level], earlier, parent)
        values.append(forward_level(level + 1, update, right_side, diag))
    solutions = [None] * 5
    partial = None
    for level in (4, 3, 2, 1, 0):
        update = backward_update(level, panels, solutions, partial, parent) if level < 4 else None
        solutions[level], partial = backward_level(
            level, update, values[level], diag, panels, solutions, parent
        )
    return assemble(solutions, right_side.shape[0])


def shards_any(right_side, reciprocal_pivot_matrix, panels, parent):
    ancestor = pair_ancestors(parent)
    return solve(right_side, reciprocal_pivot_matrix, panels, ancestor)


def solution(mesh):
    kernels = mesh.shape["leaf"] == 8 and mesh.shape["col"] == 4
    return jax.shard_map(
        shards if kernels else shards_any,
        mesh=mesh,
        in_specs=(P(None, "leaf", None), P(None, "col", "leaf"), P(None, "leaf", "col"), P()),
        out_specs=P(None, "leaf", None),
        check_vma=False,
    )
```
